32 devices in a mesh: loop: 16 (over z, y, core), lane: 2 (over x).
Axes of the slice: x: 2, y: 2, z: 4, core: 2. Of those that a mesh axis runs over, the one named last changes fastest.
Arguments:
- orbitals: bfloat16 [8192, 512], P('loop', 'lane'), may hold values from -6 to 6
- coulomb: bfloat16 [16, 2, 2, 512, 512], P('loop', 'lane'), may hold values from -0.01171875 to 0.01171875
- table: int32 [2, 2], P('lane'), may hold values from 0 to 8, as said below
Outputs:
- exchanged: bfloat16 [8192, 512], P('loop', 'lane')
The draws below stay inside these ranges and needn't reach their ends.
Inputs may be any that keep to these rules, and one draw needn't show every extreme that they name: `table`: the entries are distinct distances; 0 and 8 are always among them.
All inputs are finite; a program needn't handle non-finite values.
Results may differ from the reference program's by a relative error of at most 0.0053.
Values may be sent and summed in bfloat16 or wider, within the bound.
A program may use at most 64 MiB of HBM per device.

```python
import jax
import jax.numpy as jnp
from jax import lax

NORB = 512
PTS_GRP = 512
DPL = 2
DIST = 4
NPTS = 8192
N_LOOP = 16
N_LANE = 2


def draw_table(key, part):
    half_loop = N_LOOP // 2
    inner = jax.random.permutation(jax.random.fold_in(key, 11), half_loop - 1) + 1
    chosen = jnp.concatenate([jnp.array([0, half_loop], jnp.int32), inner[:DIST - 2].astype(jnp.int32)])
    placing = jax.random.permutation(jax.random.fold_in(key, 12), DIST)
    return chosen[placing].reshape(N_LANE, DPL).astype(jnp.int32)


def shard_levels(key, shape, pieces, least, largest):
    factor_of, own = 1.0, jax.random.fold_in(key, 6)
    for dim, parts in pieces:
        heights = jnp.exp(jax.random.uniform(jax.random.fold_in(own, dim), (parts,), jnp.float32, least / len(pieces), largest / len(pieces)))
        factor_of = factor_of * jnp.repeat(heights, shape[dim] // parts).reshape([-1 if axis == dim else 1 for axis in range(len(shape))])
    return factor_of


def scatter_about(rng, dims, scale, reach, shards=(), held_as=jnp.bfloat16):
    drawn = jax.random.normal(rng, dims, jnp.float32) * scale
    if len(shards) > 0:
        drawn = shard_levels(rng, dims, shards, -0.22, 0.18) * drawn
    return jnp.clip(drawn, min=-reach, max=reach).astype(held_as)


def setup_inputs(seed: int = 0) -> dict:
    key_of = jax.random.split(jax.random.key(seed), 4)
    orbitals = scatter_about(key_of[0], (NPTS, NORB), 1.0, 6.0, ((0, 16), (1, 2)))
    coulomb = scatter_about(key_of[1], (N_LOOP, N_LANE, DPL, PTS_GRP, PTS_GRP), (PTS_GRP * NORB) ** -0.5, 0.01171875, ((0, 16), (1, 2)))
    table = draw_table(jax.random.fold_in(key_of[3], 71), 0)
    return {"orbitals": orbitals, "coulomb": coulomb, "table": table}


def reference(orbitals, coulomb, table):
    groups = coulomb.shape[0]
    points = coulomb.shape[3]
    orbital_count = orbitals.shape[1]
    half_loop = groups // 2
    blocks = orbitals.reshape(groups, points, orbital_count).astype(jnp.float32)
    flat_table = table.reshape(-1)
    flat_coulomb = coulomb.reshape(groups, -1, points, points)
    group_ids = jnp.arange(groups, dtype=jnp.int32)

    def one_slot(summed, slot_index):
        distance = flat_table[slot_index]
        partner = jnp.take(blocks, (group_ids + distance) % groups, axis=0)
        coulomb_tile = lax.dynamic_index_in_dim(flat_coulomb, slot_index, 1, keepdims=False).astype(jnp.float32)
        gram_tile = jnp.einsum("agn,ahn->agh", blocks, partner)
        rounded = (coulomb_tile * gram_tile).astype(jnp.bfloat16)
        rounded = lax.optimization_barrier(rounded)
        pair_tile = rounded.astype(jnp.float32)
        direct = jnp.einsum("agh,ahn->agn", pair_tile, partner)
        weight = jnp.logical_and(distance > 0, distance < half_loop).astype(jnp.float32)
        back_term = (jnp.einsum("agh,agn->ahn", pair_tile, blocks) * weight).astype(jnp.bfloat16)
        arrived = jnp.take(back_term, (group_ids - distance) % groups, axis=0)
        return summed + direct + arrived.astype(jnp.float32), None

    start = jnp.zeros((groups, points, orbital_count), jnp.float32)
    summed, _ = lax.scan(one_slot, start, jnp.arange(flat_table.shape[0], dtype=jnp.int32))
    return summed.reshape(groups * points, orbital_count).astype(jnp.bfloat16)
```

```python
import functools

import jax
import jax.numpy as jnp
from jax import lax
from jax.experimental import pallas as pl
from jax.experimental.pallas import tpu as pltpu
from jax.sharding import PartitionSpec as P

PIECES = 2
MESH = pl.DeviceIdType.MESH


def from_behind(shard, axis, by):
    peers = lax.axis_size(axis)
    return lax.ppermute(shard, axis, [(i, (i + by) % peers) for i in range(peers)])


def select_bits(shifted, current, distances, level):
    chosen = distances >> level & 1 == 1
    return jnp.where(chosen[:, None, None], shifted, current)


def general_body(orbitals, coulomb, table):
    own_slab = lax.all_gather(orbitals, "lane", axis=1, tiled=True)
    half_loop = lax.axis_size("loop") // 2
    bit_count = half_loop.bit_length()
    slot_count = coulomb.shape[2]
    own_dists = table[0]
    first_move = from_behind(own_slab, "loop", -1)
    fetched = select_bits(first_move[None], own_slab[None], own_dists, 0)
    for level in range(1, bit_count):
        shifted = from_behind(fetched, "loop", -(1 << level))
        fetched = select_bits(shifted, fetched, own_dists, level)
    direct = jnp.zeros(own_slab.shape, jnp.float32)
    back_list = []
    for slot in range(slot_count):
        partner = fetched[slot]
        gram_tile = lax.dot_general(
            own_slab, partner, (((1,), (1,)), ((), ())), preferred_element_type=jnp.float32
        )
        pair_tile = (coulomb[0, 0, slot].astype(jnp.float32) * gram_tile).astype(jnp.bfloat16)
        direct = direct + jnp.dot(pair_tile, partner, preferred_element_type=jnp.float32)
        distance = own_dists[slot]
        weight = jnp.logical_and(distance > 0, distance < half_loop).astype(jnp.float32)
        back_value = lax.dot_general(
            pair_tile, own_slab, (((0,), (0,)), ((), ())), preferred_element_type=jnp.float32
        )
        back_list.append((back_value * weight).astype(jnp.bfloat16))
    back_terms = jnp.stack(back_list)
    for level in range(bit_count - 1):
        shifted = from_behind(back_terms, "loop", 1 << level)
        back_terms = select_bits(shifted, back_terms, own_dists, level)
    summed = direct + jnp.sum(back_terms.astype(jnp.float32), axis=0)
    result = lax.psum_scatter(summed, "lane", scatter_dimension=1, tiled=True)
    return result.astype(jnp.bfloat16)


def pick(items, index):
    value = items[-1]
    for i in range(len(items) - 2, -1, -1):
        value = jnp.where(index == i, items[i], value)
    return value


def kernel(
    n_loop, h_ref, c_ref, t_ref, out_ref,
    slab, tiles, tab_out, tab_in, pools, y_out, sel, b_out, b_in,
    same, core_out, core_in, z_out, z_in, x_out, x_in, direct, d_out, d_in,
    stack, fin, send, recv, local,
):
    half_loop = n_loop // 2
    me = lax.axis_index("loop")
    x = lax.axis_index("lane")
    ox = 1 - x
    c = me % 2
    y = (me // 2) % 2
    z4 = (me // 4) * 4
    low = me - z4
    points, width = h_ref.shape
    rows = points // 2
    chunk = rows // PIECES
    bf16, f32 = jnp.bfloat16, jnp.float32

    def at_z(step):
        return ((z4 + 4 * step) % n_loop + low, x)

    across = (me, ox)
    core = (me + 1 - 2 * c, x)
    over_y = (me + 2 - 4 * y, x)

    counter = [0]

    def remote(src, dst, to):
        i = counter[0]
        counter[0] += 1
        copy = pltpu.make_async_remote_copy(
            src_ref=src, dst_ref=dst, send_sem=send.at[i], recv_sem=recv.at[i],
            device_id=to, device_id_type=MESH,
        )
        copy.start()
        started.append(copy)
        return copy

    started = []

    barrier = pltpu.get_barrier_semaphore()
    for peer in (across, core, over_y, at_z(1), at_z(2), at_z(3)):
        pl.semaphore_signal(barrier, inc=1, device_id=peer, device_id_type=MESH)
    pl.semaphore_wait(barrier, 6)

    my_cols = pl.ds(pl.multiple_of(x * width, width), width)
    other_cols = pl.ds(pl.multiple_of(ox * width, width), width)
    my_rows = pl.ds(pl.multiple_of(x * rows, rows), rows)
    other_rows = pl.ds(pl.multiple_of(ox * rows, rows), rows)

    def my_chunk(k):
        return pl.ds(pl.multiple_of(x * rows + k * chunk, chunk), chunk)

    def other_chunk(k):
        return pl.ds(pl.multiple_of(ox * rows + k * chunk, chunk), chunk)

    piece_in = [
        remote(h_ref.at[other_chunk(k)], pools[k].at[c, :, my_cols], across)
        for k in range(PIECES)
    ]
    for s in range(2):
        tab_out[s] = jnp.full(tab_out.shape[1:], t_ref[0, s], jnp.int32)
    table_in = remote(tab_out, tab_in, across)
    for k in range(PIECES):
        pools[k][c, :, my_cols] = h_ref[my_chunk(k)]
    slab_in = remote(h_ref.at[my_rows], slab.at[my_rows, my_cols], across)
    tile_in = [
        remote(c_ref.at[0, 0, s, :, other_cols], tiles.at[2 * x + s], across) for s in range(2)
    ]
    tile_own = []
    for s in range(2):
        copy = pltpu.make_async_copy(c_ref.at[0, 0, s, :, my_cols], tiles.at[2 * x + s], local.at[s])
        copy.start()
        tile_own.append(copy)

    z_move, core_move = [], []
    for k in range(PIECES):
        piece_in[k].wait_recv()
        z_move.append([
            remote(pools[k].at[c], pools[k].at[2 * step + c], at_z(4 - step)) for step in (1, 2)
        ])
        core_move.append([remote(pools[k].at[c], pools[k].at[c], core)])

    slab[other_rows, my_cols] = h_ref[other_rows]
    for k in range(PIECES):
        slab[my_chunk(k), :] = pools[k][c]

    table_in.wait_recv()
    mine = [t_ref[0, s] for s in range(2)]
    theirs = [jnp.max(tab_in[s]) for s in range(2)]
    first = x == 0
    dist = [jnp.where(first, mine[s], theirs[s]) for s in range(2)]
    dist += [jnp.where(first, theirs[s], mine[s]) for s in range(2)]
    inner = [jnp.logical_and(d != 0, d != half_loop) for d in dist]
    slot_zero = pick([jnp.int32(i) for i in range(4)], jnp.int32(-1))
    slot_half = slot_zero
    for i in range(3):
        slot_zero = jnp.where(dist[i] == 0, i, slot_zero)
        slot_half = jnp.where(dist[i] == half_loop, i, slot_half)
    slot_a = jnp.where(inner[0], 0, jnp.where(inner[1], 1, 2))
    slot_b = jnp.where(inner[3], 3, jnp.where(inner[2], 2, 1))
    inner_slots = (slot_a, slot_b)
    inner_dist = [pick(dist, s) for s in inner_slots]
    own_at = [low + d for d in inner_dist]
    next_at = [low + 2 - 4 * y + d for d in inner_dist]

    def spot(at):
        return (at >> 2) * 2 + (at & 1)

    def here(at):
        return ((at >> 1) & 1) ^ y

    y_move = []
    for k in range(PIECES):
        for step in (1, 2):
            z_move[k][step - 1].wait_recv()
            core_move[k].append(
                remote(pools[k].at[2 * step + c], pools[k].at[2 * step + c], core)
            )
        for copy in core_move[k]:
            copy.wait_recv()
        for j in range(2):
            y_out[k][j] = pools[k][spot(next_at[j])]
        y_move.append(remote(y_out[k], sel[k].at[pl.ds(2, 2)], over_y))
        for j in range(2):
            sel[k][j] = pools[k][spot(own_at[j])]

    slab_in.wait_recv()
    for copy in tile_own:
        copy.wait()
    for copy in tile_in:
        copy.wait_recv()

    b_move = []
    for k in range(PIECES):
        stack[pl.ds(0, chunk)] = pools[k][c]
        stack[pl.ds(chunk, chunk)] = pools[k][4 + c]
        y_move[k].wait_recv()
        for j in range(2):
            stack[pl.ds((2 + j) * chunk, chunk)] = sel[k][j + 2 * here(own_at[j])]
        gram = lax.dot_general(
            slab[...], stack[...], (((1,), (1,)), ((), ())), preferred_element_type=f32
        )
        held = jnp.concatenate(
            [tiles[s, :, pl.ds(k * chunk, chunk)] for s in (slot_zero, slot_half) + inner_slots],
            axis=1,
        )
        pair = (held.astype(f32) * gram).astype(bf16)
        back = lax.dot_general(
            pair[:, 2 * chunk:], slab[...], (((0,), (0,)), ((), ())), preferred_element_type=f32
        ).astype(bf16)
        for j in range(2):
            b_out[k][j] = back[j * chunk:(j + 1) * chunk]
        b_move.append(remote(b_out[k], b_in[k], over_y))
        part = jnp.dot(pair, stack[...], preferred_element_type=f32)
        if k == 0:
            direct[...] = part
        else:
            direct[...] += part
    d_out[...] = direct[:, other_cols].astype(bf16)
    direct_move = remote(d_out, d_in, across)

    def mask(at, plane, side):
        fits = jnp.logical_and(here(at) == 0, spot(at) == plane * 2 + side)
        return jnp.where(fits, 1.0, 0.0).astype(f32)

    b_core, b_z = [], []
    for k in range(PIECES):
        b_move[k].wait_recv()
        for plane in range(3):
            keep = jnp.zeros((chunk, 2 * width), f32)
            give = jnp.zeros((chunk, 2 * width), f32)
            for j in range(2):
                for at, src in ((own_at[j], b_out[k]), (next_at[j], b_in[k])):
                    value = src[j].astype(f32)
                    keep += value * mask(at, plane, c)
                    give += value * mask(at, plane, 1 - c)
            same[k][plane] = keep
            core_out[k][plane] = give.astype(bf16)
        b_core.append(remote(core_out[k], core_in[k], core))
    for k in range(PIECES):
        b_core[k].wait_recv()
        moves = []
        for step in (2, 1):
            z_out[k][step - 1] = (same[k][step] + core_in[k][step].astype(f32)).astype(bf16)
            moves.append(remote(z_out[k].at[step - 1], z_in[k].at[step - 1], at_z(step)))
        b_z.append(moves)
    last = []
    for k in range(PIECES):
        for copy in b_z[k]:
            copy.wait_recv()
        fin[k] = (
            same[k][0] + core_in[k][0].astype(f32)
            + z_in[k][0].astype(f32) + z_in[k][1].astype(f32)
        )
        x_out[k][...] = fin[k, :, other_cols].astype(bf16)
        last.append(remote(x_out[k], x_in[k], across))
    direct_move.wait_recv()
    for k in range(PIECES):
        r = my_chunk(k)
        out_ref[r, :] = (
            direct[r, my_cols] + d_in[r, :].astype(f32) + fin[k, :, my_cols]
        ).astype(bf16)
    for k in range(PIECES):
        last[k].wait_recv()
        r = other_chunk(k)
        out_ref[r, :] = (
            direct[r, my_cols] + d_in[r, :].astype(f32) + x_in[k][...].astype(f32)
        ).astype(bf16)
    for copy in started:
        copy.wait_send()


COPIES = 4 + 1 + 12 * PIECES


def planned_body(n_loop, orbitals, coulomb, table):
    points, width = orbitals.shape
    rows, full = points // 2, 2 * width
    chunk = rows // PIECES
    bf16, f32 = jnp.bfloat16, jnp.float32

    def each(shape, dtype=bf16):
        return [pltpu.VMEM(shape, dtype) for _ in range(PIECES)]

    return pl.pallas_call(
        functools.partial(kernel, n_loop),
        out_shape=jax.ShapeDtypeStruct(orbitals.shape, bf16),
        in_specs=[
            pl.BlockSpec(memory_space=pltpu.VMEM),
            pl.BlockSpec(memory_space=pltpu.VMEM),
            pl.BlockSpec(memory_space=pltpu.SMEM),
        ],
        out_specs=pl.BlockSpec(memory_space=pltpu.VMEM),
        scratch_shapes=[
            pltpu.VMEM((points, full), bf16),
            pltpu.VMEM((4, points, rows), bf16),
            pltpu.VMEM((2, 8, 128), jnp.int32),
            pltpu.VMEM((2, 8, 128), jnp.int32),
            each((6, chunk, full)),
            each((2, chunk, full)),
            each((4, chunk, full)),
            each((2, chunk, full)),
            each((2, chunk, full)),
            each((3, chunk, full), f32),
            each((3, chunk, full)),
            each((3, chunk, full)),
            each((2, chunk, full)),
            each((2, chunk, full)),
            each((chunk, width)),
            each((chunk, width)),
            pltpu.VMEM((points, full), f32),
            pltpu.VMEM((points, width), bf16),
            pltpu.VMEM((points, width), bf16),
            pltpu.VMEM((4 * chunk, full), bf16),
            pltpu.VMEM((PIECES, chunk, full), f32),
            pltpu.SemaphoreType.DMA((COPIES,)),
            pltpu.SemaphoreType.DMA((COPIES,)),
            pltpu.SemaphoreType.DMA((2,)),
        ],
        compiler_params=pltpu.CompilerParams(
            collective_id=0, has_side_effects=True, vmem_limit_bytes=48 * 1024 * 1024
        ),
    )(orbitals, coulomb, table)


def solution(mesh):
    in_specs = (P("loop", "lane"), P("loop", "lane", None, None, None), P("lane", None))
    out_specs = P("loop", "lane")
    n_loop, n_lane = mesh.shape["loop"], mesh.shape["lane"]
    fits = n_loop == 4 * 4 and n_lane == 2
    body = functools.partial(planned_body, n_loop) if fits else general_body
    return jax.shard_map(body, mesh=mesh, in_specs=in_specs, out_specs=out_specs, check_vma=False)
```

```python
import functools

import jax
import jax.numpy as jnp
from jax import lax
from jax.experimental import pallas as pl
from jax.experimental.pallas import tpu as pltpu
from jax.sharding import PartitionSpec as P

PIECES = 4
PARTS = 2
MESH = pl.DeviceIdType.MESH


def from_behind(shard, axis, by):
    peers = lax.axis_size(axis)
    return lax.ppermute(shard, axis, [(i, (i + by) % peers) for i in range(peers)])


def select_bits(shifted, current, distances, level):
    chosen = distances >> level & 1 == 1
    return jnp.where(chosen[:, None, None], shifted, current)


def general_body(orbitals, coulomb, table):
    own_slab = lax.all_gather(orbitals, "lane", axis=1, tiled=True)
    half_loop = lax.axis_size("loop") // 2
    bit_count = half_loop.bit_length()
    slot_count = coulomb.shape[2]
    own_dists = table[0]
    first_move = from_behind(own_slab, "loop", -1)
    fetched = select_bits(first_move[None], own_slab[None], own_dists, 0)
    for level in range(1, bit_count):
        shifted = from_behind(fetched, "loop", -(1 << level))
        fetched = select_bits(shifted, fetched, own_dists, level)
    direct = jnp.zeros(own_slab.shape, jnp.float32)
    back_list = []
    for slot in range(slot_count):
        partner = fetched[slot]
        gram_tile = lax.dot_general(
            own_slab, partner, (((1,), (1,)), ((), ())), preferred_element_type=jnp.float32
        )
        pair_tile = (coulomb[0, 0, slot].astype(jnp.float32) * gram_tile).astype(jnp.bfloat16)
        direct = direct + jnp.dot(pair_tile, partner, preferred_element_type=jnp.float32)
        distance = own_dists[slot]
        weight = jnp.logical_and(distance > 0, distance < half_loop).astype(jnp.float32)
        back_value = lax.dot_general(
            pair_tile, own_slab, (((0,), (0,)), ((), ())), preferred_element_type=jnp.float32
        )
        back_list.append((back_value * weight).astype(jnp.bfloat16))
    back_terms = jnp.stack(back_list)
    for level in range(bit_count - 1):
        shifted = from_behind(back_terms, "loop", 1 << level)
        back_terms = select_bits(shifted, back_terms, own_dists, level)
    summed = direct + jnp.sum(back_terms.astype(jnp.float32), axis=0)
    result = lax.psum_scatter(summed, "lane", scatter_dimension=1, tiled=True)
    return result.astype(jnp.bfloat16)


def pick(items, index):
    value = items[-1]
    for i in range(len(items) - 2, -1, -1):
        value = jnp.where(index == i, items[i], value)
    return value


def kernel(
    n_loop, h_ref, c_ref, t_ref, out_ref,
    slab, tiles, tab_out, tab_in, pools, y_out, sel, cand,
    same, core_out, core_in, z_out, z_in, z_via, x_out, x_in, direct, d_out, d_in,
    stack, fin, send, recv, local,
):
    half_loop = n_loop // 2
    me = lax.axis_index("loop")
    x = lax.axis_index("lane")
    ox = 1 - x
    c = me % 2
    y = (me // 2) % 2
    z = me // 4
    low = me - z * 4
    points, width = h_ref.shape
    rows = points // 2
    chunk = rows // PIECES
    part_cols = rows // PARTS
    per_part = PIECES // PARTS
    bf16, f32 = jnp.bfloat16, jnp.float32

    def at_z(step):
        return ((z * 4 + 4 * step) % n_loop + low, x)

    across = (me, ox)
    core = (me + 1 - 2 * c, x)
    over_y = (me + 2 - 4 * y, x)

    sems = {}

    def sem_of(name):
        return sems.setdefault(name, len(sems))

    started = []

    def remote(name, src, dst, to, lands=None, when=None):
        copy = pltpu.make_async_remote_copy(
            src_ref=src, dst_ref=dst, send_sem=send.at[sem_of(name)],
            recv_sem=recv.at[sem_of(lands or name)], device_id=to, device_id_type=MESH,
        )
        if when is None:
            copy.start()
        else:
            pl.when(when)(copy.start)
        started.append((copy, when))
        return copy

    my_cols = pl.ds(pl.multiple_of(x * width, width), width)
    other_cols = pl.ds(pl.multiple_of(ox * width, width), width)
    my_rows = pl.ds(pl.multiple_of(x * rows, rows), rows)
    other_rows = pl.ds(pl.multiple_of(ox * rows, rows), rows)

    def my_chunk(k):
        return pl.ds(pl.multiple_of(x * rows + k * chunk, chunk), chunk)

    def other_chunk(k):
        return pl.ds(pl.multiple_of(ox * rows + k * chunk, chunk), chunk)

    def tile_cols(half, lane):
        return pl.ds(pl.multiple_of(lane * rows + half * part_cols, part_cols), part_cols)

    own_copies, slab_own = [], []
    for k in range(PIECES):
        copy = pltpu.make_async_copy(
            h_ref.at[my_chunk(k)], pools[k].at[c, :, my_cols], local.at[k]
        )
        copy.start()
        own_copies.append(copy)
    copy = pltpu.make_async_copy(h_ref, slab.at[:, my_cols], local.at[PIECES])
    copy.start()
    slab_own.append(copy)
    for half in range(PARTS):
        for s in range(2):
            copy = pltpu.make_async_copy(
                c_ref.at[0, 0, s, :, tile_cols(half, x)], tiles[half].at[2 * x + s],
                local.at[PIECES + 1 + 2 * half + s],
            )
            copy.start()
            slab_own.append(copy)
    for s in range(2):
        tab_out[s] = jnp.full(tab_out.shape[1:], t_ref[0, s], jnp.int32)
    for k in range(PIECES):
        cand[k][4] = jnp.zeros(cand[k].shape[1:], bf16)

    @pl.when(z == 0)
    def _():
        for k in range(PIECES):
            z_in[k][0] = jnp.zeros(z_in[k].shape[1:], bf16)

    @pl.when(z == 2)
    def _():
        for k in range(PIECES):
            z_in[k][1] = jnp.zeros(z_in[k].shape[1:], bf16)

    barrier = pltpu.get_barrier_semaphore()
    for peer in (across, core, over_y, at_z(1), at_z(2), at_z(3)):
        pl.semaphore_signal(barrier, inc=1, device_id=peer, device_id_type=MESH)
    pl.semaphore_wait(barrier, 6)

    piece_in = [
        remote(("piece", k), h_ref.at[other_chunk(k)], pools[k].at[c, :, my_cols], across)
        for k in range(PIECES)
    ]
    table_in = remote(("table",), tab_out, tab_in, across)

    z_move, core_move = [], []
    for k in range(PIECES):
        own_copies[k].wait()
        piece_in[k].wait_recv()
        one = remote(
            ("z1", k), pools[k].at[c], pools[k].at[2 + c], at_z(3), when=z != 0
        )
        two = remote(
            ("z2", k), pools[k].at[c], pools[k].at[4 + c], at_z(2), when=z != 2
        )
        z_move.append((one, two))
        core_move.append([remote(("c0", k), pools[k].at[c], pools[k].at[c], core)])
    slab_in = remote(("slab",), h_ref.at[my_rows], slab.at[my_rows, my_cols], across)

    def send_tiles(half):
        return [
            remote(
                ("tile", half, s), c_ref.at[0, 0, s, :, tile_cols(half, ox)],
                tiles[half].at[2 * x + s], across,
            )
            for s in range(2)
        ]

    tile_in = [send_tiles(half) for half in range(1)]

    table_in.wait_recv()
    mine = [t_ref[0, s] for s in range(2)]
    theirs = [jnp.max(tab_in[s]) for s in range(2)]
    first = x == 0
    dist = [jnp.where(first, mine[s], theirs[s]) for s in range(2)]
    dist += [jnp.where(first, theirs[s], mine[s]) for s in range(2)]
    inner = [jnp.logical_and(d != 0, d != half_loop) for d in dist]
    slot_zero = jnp.int32(3)
    slot_half = slot_zero
    for i in range(3):
        slot_zero = jnp.where(dist[i] == 0, i, slot_zero)
        slot_half = jnp.where(dist[i] == half_loop, i, slot_half)
    slot_a = jnp.where(inner[0], 0, jnp.where(inner[1], 1, 2))
    slot_b = jnp.where(inner[3], 3, jnp.where(inner[2], 2, 1))
    inner_slots = (slot_a, slot_b)
    inner_dist = [pick(dist, s) for s in inner_slots]
    own_at = [low + d for d in inner_dist]
    next_at = [low + 2 - 4 * y + d for d in inner_dist]

    def spot(at):
        return (at >> 2) * 2 + (at & 1)

    def here(at):
        return ((at >> 1) & 1) ^ y

    def source(j, plane, side):
        want = plane * 2 + side
        own = jnp.logical_and(here(own_at[j]) == 0, spot(own_at[j]) == want)
        near = jnp.logical_and(here(next_at[j]) == 0, spot(next_at[j]) == want)
        return jnp.where(own, j, jnp.where(near, 2 + j, 4))

    y_move, b_move, b_core, b_z, last = [], [], [], [], []

    def gather_rows(k):
        for step in (1, 2):
            z_move[k][step - 1].wait_recv()
            if step == 1:
                remote(
                    ("via1", k), pools[k].at[2 + c], pools[k].at[4 + c], at_z(3),
                    lands=("z2", k), when=z == 1,
                )
            else:
                remote(
                    ("via2", k), pools[k].at[4 + c], pools[k].at[2 + c], at_z(1),
                    lands=("z1", k), when=z == 2,
                )
            core_move[k].append(
                remote(
                    ("c", step, k), pools[k].at[2 * step + c], pools[k].at[2 * step + c], core
                )
            )
        for copy in core_move[k]:
            copy.wait_recv()
        for j in range(2):
            y_out[k][j] = pools[k][spot(next_at[j])]
        y_move.append(remote(("y", k), y_out[k], sel[k].at[pl.ds(2, 2)], over_y))
        for j in range(2):
            sel[k][j] = pools[k][spot(own_at[j])]

    def compute(k):
        half = k // per_part
        if k == 0:
            for copy in slab_own:
                copy.wait()
            for i in range(PIECES):
                slab[my_chunk(i), other_cols] = pools[i][c, :, other_cols]
            slab_in.wait_recv()
        if k % per_part == 0:
            for copy in tile_in[half]:
                copy.wait_recv()
        stack[pl.ds(0, chunk)] = pools[k][c]
        stack[pl.ds(chunk, chunk)] = pools[k][4 + c]
        y_move[k].wait_recv()
        for j in range(2):
            stack[pl.ds((2 + j) * chunk, chunk)] = sel[k][j + 2 * here(own_at[j])]
        gram = lax.dot_general(
            slab[...], stack[...], (((1,), (1,)), ((), ())), preferred_element_type=f32
        )
        at = (k % per_part) * chunk
        held = jnp.concatenate(
            [tiles[half][s, :, at:at + chunk] for s in (slot_zero, slot_half) + inner_slots],
            axis=1,
        )
        pair = (held.astype(f32) * gram).astype(bf16)
        back = lax.dot_general(
            pair[:, 2 * chunk:], slab[...], (((0,), (0,)), ((), ())), preferred_element_type=f32
        ).astype(bf16)
        for j in range(2):
            cand[k][j] = back[j * chunk:(j + 1) * chunk]
        b_move.append(
            remote(("b", k), cand[k].at[pl.ds(0, 2)], cand[k].at[pl.ds(2, 2)], over_y)
        )
        part = jnp.dot(pair, stack[...], preferred_element_type=f32)
        if k == 0:
            direct[...] = part
        else:
            direct[...] += part
        if k == PIECES - 1:
            d_out[...] = direct[:, other_cols].astype(bf16)
            last.append(remote(("direct",), d_out, d_in, across))

    def sort_back(k):
        b_move[k].wait_recv()
        for plane in (2, 1, 0):
            for side, keep in ((1 - c, False), (c, True)):
                a, b = (cand[k][source(j, plane, side)].astype(f32) for j in range(2))
                if keep:
                    same[k][plane] = a + b
                else:
                    core_out[k][plane] = (a + b).astype(bf16)
        b_core.append(remote(("bc", k), core_out[k], core_in[k], core))

    def send_back(k):
        b_core[k].wait_recv()

        def total(step):
            return same[k][step] + core_in[k][step].astype(f32)

        for step in (1, 2):
            z_out[k][step - 1] = total(step).astype(bf16)
        one, two = z_out[k].at[0], z_out[k].at[1]
        via = remote(("v0", k), two, z_via[k], at_z(1), lands=("v", k), when=z == 0)
        remote(("v3", k), one, z_via[k], at_z(3), lands=("v", k), when=z == 3)
        z_a = remote(
            ("ba", k), one, z_in[k].at[0], at_z(1), lands=("bz1", k),
            when=jnp.logical_or(z == 0, z == 2),
        )
        z_b = remote(
            ("bb", k), two, z_in[k].at[1], at_z(2), lands=("bz2", k),
            when=jnp.logical_or(z == 1, z == 3),
        )

        @pl.when(z == 1)
        def _():
            via.wait_recv()
            z_out[k][0] = (total(1) + z_via[k][...].astype(f32)).astype(bf16)

        @pl.when(z == 2)
        def _():
            via.wait_recv()
            z_out[k][1] = (total(2) + z_via[k][...].astype(f32)).astype(bf16)

        remote(("bc1", k), one, z_in[k].at[0], at_z(1), lands=("bz1", k), when=z == 1)
        remote(("bc2", k), two, z_in[k].at[1], at_z(2), lands=("bz2", k), when=z == 2)
        b_z.append((z_a, z_b))

    def finish(k):
        pl.when(z != 0)(b_z[k][0].wait_recv)
        pl.when(z != 2)(b_z[k][1].wait_recv)
        fin[k] = (
            same[k][0] + core_in[k][0].astype(f32)
            + z_in[k][0].astype(f32) + z_in[k][1].astype(f32)
        )
        x_out[k][...] = fin[k, :, other_cols].astype(bf16)
        last.append(remote(("x", k), x_out[k], x_in[k], across))

    for t in range(PIECES + 4):
        for lag, step in enumerate((gather_rows, compute, sort_back, send_back, finish)):
            if 0 <= t - lag < PIECES:
                step(t - lag)
        if t + 1 < PARTS:
            tile_in.append(send_tiles(t + 1))

    last[0].wait_recv()
    for k in range(PIECES):
        r = my_chunk(k)
        out_ref[r, :] = (
            direct[r, my_cols] + d_in[r, :].astype(f32) + fin[k, :, my_cols]
        ).astype(bf16)
    for k in range(PIECES):
        last[k + 1].wait_recv()
        r = other_chunk(k)
        out_ref[r, :] = (
            direct[r, my_cols] + d_in[r, :].astype(f32) + x_in[k][...].astype(f32)
        ).astype(bf16)
    for copy, when in started:
        if when is None:
            copy.wait_send()
        else:
            pl.when(when)(copy.wait_send)


COPIES = 3 + 2 * PARTS + 24 * PIECES


def planned_body(n_loop, orbitals, coulomb, table):
    points, width = orbitals.shape
    rows, full = points // 2, 2 * width
    chunk = rows // PIECES
    bf16, f32 = jnp.bfloat16, jnp.float32

    def each(shape, dtype=bf16, count=PIECES):
        return [pltpu.VMEM(shape, dtype) for _ in range(count)]

    return pl.pallas_call(
        functools.partial(kernel, n_loop),
        out_shape=jax.ShapeDtypeStruct(orbitals.shape, bf16),
        in_specs=[
            pl.BlockSpec(memory_space=pltpu.HBM),
            pl.BlockSpec(memory_space=pltpu.HBM),
            pl.BlockSpec(memory_space=pltpu.SMEM),
        ],
        out_specs=pl.BlockSpec(memory_space=pltpu.VMEM),
        scratch_shapes=[
            pltpu.VMEM((points, full), bf16),
            each((4, points, rows // PARTS), count=PARTS),
            pltpu.VMEM((2, 8, 128), jnp.int32),
            pltpu.VMEM((2, 8, 128), jnp.int32),
            each((6, chunk, full)),
            each((2, chunk, full)),
            each((4, chunk, full)),
            each((5, chunk, full)),
            each((3, chunk, full), f32),
            each((3, chunk, full)),
            each((3, chunk, full)),
            each((2, chunk, full)),
            each((2, chunk, full)),
            each((chunk, full)),
            each((chunk, width)),
            each((chunk, width)),
            pltpu.VMEM((points, full), f32),
            pltpu.VMEM((points, width), bf16),
            pltpu.VMEM((points, width), bf16),
            pltpu.VMEM((4 * chunk, full), bf16),
            pltpu.VMEM((PIECES, chunk, full), f32),
            pltpu.SemaphoreType.DMA((COPIES,)),
            pltpu.SemaphoreType.DMA((COPIES,)),
            pltpu.SemaphoreType.DMA((PIECES + 1 + 2 * PARTS,)),
        ],
        compiler_params=pltpu.CompilerParams(
            collective_id=0, has_side_effects=True, vmem_limit_bytes=63 * 1024 * 1024
        ),
    )(orbitals, coulomb, table)


def solution(mesh):
    in_specs = (P("loop", "lane"), P("loop", "lane", None, None, None), P("lane", None))
    out_specs = P("loop", "lane")
    n_loop, n_lane = mesh.shape["loop"], mesh.shape["lane"]
    fits = n_loop == 4 * 4 and n_lane == 2
    body = functools.partial(planned_body, n_loop) if fits else general_body
    return jax.shard_map(body, mesh=mesh, in_specs=in_specs, out_specs=out_specs, check_vma=False)
```

```python
import functools

import jax
import jax.numpy as jnp
from jax import lax
from jax.experimental import pallas as pl
from jax.experimental.pallas import tpu as pltpu
from jax.sharding import PartitionSpec as P

PIECES = 4
RELAYED = ()
AHEAD = 2
PARTS = 2
MESH = pl.DeviceIdType.MESH


def from_behind(shard, axis, by):
    peers = lax.axis_size(axis)
    return lax.ppermute(shard, axis, [(i, (i + by) % peers) for i in range(peers)])


def select_bits(shifted, current, distances, level):
    chosen = distances >> level & 1 == 1
    return jnp.where(chosen[:, None, None], shifted, current)


def general_body(orbitals, coulomb, table):
    own_slab = lax.all_gather(orbitals, "lane", axis=1, tiled=True)
    half_loop = lax.axis_size("loop") // 2
    bit_count = half_loop.bit_length()
    slot_count = coulomb.shape[2]
    own_dists = table[0]
    first_move = from_behind(own_slab, "loop", -1)
    fetched = select_bits(first_move[None], own_slab[None], own_dists, 0)
    for level in range(1, bit_count):
        shifted = from_behind(fetched, "loop", -(1 << level))
        fetched = select_bits(shifted, fetched, own_dists, level)
    direct = jnp.zeros(own_slab.shape, jnp.float32)
    back_list = []
    for slot in range(slot_count):
        partner = fetched[slot]
        gram_tile = lax.dot_general(
            own_slab, partner, (((1,), (1,)), ((), ())), preferred_element_type=jnp.float32
        )
        pair_tile = (coulomb[0, 0, slot].astype(jnp.float32) * gram_tile).astype(jnp.bfloat16)
        direct = direct + jnp.dot(pair_tile, partner, preferred_element_type=jnp.float32)
        distance = own_dists[slot]
        weight = jnp.logical_and(distance > 0, distance < half_loop).astype(jnp.float32)
        back_value = lax.dot_general(
            pair_tile, own_slab, (((0,), (0,)), ((), ())), preferred_element_type=jnp.float32
        )
        back_list.append((back_value * weight).astype(jnp.bfloat16))
    back_terms = jnp.stack(back_list)
    for level in range(bit_count - 1):
        shifted = from_behind(back_terms, "loop", 1 << level)
        back_terms = select_bits(shifted, back_terms, own_dists, level)
    summed = direct + jnp.sum(back_terms.astype(jnp.float32), axis=0)
    result = lax.psum_scatter(summed, "lane", scatter_dimension=1, tiled=True)
    return result.astype(jnp.bfloat16)


def pick(items, index):
    value = items[-1]
    for i in range(len(items) - 2, -1, -1):
        value = jnp.where(index == i, items[i], value)
    return value


def kernel(
    n_loop, h_ref, c_ref, t_ref, out_ref,
    slab, tiles, tab_out, tab_in, pools, y_out, sel, cand,
    same, core_out, core_in, z_out, z_in, direct, d_out, d_in, stack, send, recv, local,
):
    half_loop = n_loop // 2
    me = lax.axis_index("loop")
    x = lax.axis_index("lane")
    ox = 1 - x
    c = me % 2
    y = (me // 2) % 2
    z = me // 4
    low = me - z * 4
    points, width = h_ref.shape
    rows = points // 2
    chunk = rows // PIECES
    part_cols = rows // PARTS
    per_part = PIECES // PARTS
    bf16, f32 = jnp.bfloat16, jnp.float32

    def at_z(step):
        return ((z * 4 + 4 * step) % n_loop + low, x)

    across = (me, ox)
    core = (me + 1 - 2 * c, x)
    over_y = (me + 2 - 4 * y, x)

    sems = {}

    def sem_of(name):
        return sems.setdefault(name, len(sems))

    started = []

    def remote(name, src, dst, to, lands=None, when=None):
        copy = pltpu.make_async_remote_copy(
            src_ref=src, dst_ref=dst, send_sem=send.at[sem_of(name)],
            recv_sem=recv.at[sem_of(lands or name)], device_id=to, device_id_type=MESH,
        )
        if when is None:
            copy.start()
        else:
            pl.when(when)(copy.start)
        started.append((copy, when))
        return copy

    my_cols = pl.ds(pl.multiple_of(x * width, width), width)
    other_cols = pl.ds(pl.multiple_of(ox * width, width), width)
    my_rows = pl.ds(pl.multiple_of(x * rows, rows), rows)
    other_rows = pl.ds(pl.multiple_of(ox * rows, rows), rows)

    def my_chunk(k):
        return pl.ds(pl.multiple_of(x * rows + k * chunk, chunk), chunk)

    def other_chunk(k):
        return pl.ds(pl.multiple_of(ox * rows + k * chunk, chunk), chunk)

    def tile_cols(half, lane):
        return pl.ds(pl.multiple_of(lane * rows + half * part_cols, part_cols), part_cols)

    own_copies, slab_own = [], []
    for k in range(PIECES):
        copy = pltpu.make_async_copy(
            h_ref.at[my_chunk(k)], pools[k].at[c, :, my_cols], local.at[k]
        )
        copy.start()
        own_copies.append(copy)
    copy = pltpu.make_async_copy(h_ref, slab.at[:, my_cols], local.at[PIECES])
    copy.start()
    slab_own.append(copy)
    for half in range(PARTS):
        for s in range(2):
            copy = pltpu.make_async_copy(
                c_ref.at[0, 0, s, :, tile_cols(half, x)], tiles[half].at[2 * x + s],
                local.at[PIECES + 1 + 2 * half + s],
            )
            copy.start()
            slab_own.append(copy)
    for s in range(2):
        tab_out[s] = jnp.full(tab_out.shape[1:], t_ref[0, s], jnp.int32)
    for k in range(PIECES):
        cand[k][4] = jnp.zeros(cand[k].shape[1:], bf16)

    barrier = pltpu.get_barrier_semaphore()
    peers = [across, core, over_y]
    peers += [(at_z(step)[0], lane) for step in (1, 2, 3) for lane in (x, ox)]
    for peer in peers:
        pl.semaphore_signal(barrier, inc=1, device_id=peer, device_id_type=MESH)
    pl.semaphore_wait(barrier, len(peers))

    piece_in = [
        remote(("piece", k), h_ref.at[other_chunk(k)], pools[k].at[c, :, my_cols], across)
        for k in range(PIECES)
    ]
    table_in = remote(("table",), tab_out, tab_in, across)

    z_move, core_move = [], []

    def send_rows(k):
        own_copies[k].wait()
        piece_in[k].wait_recv()
        one = remote(
            ("z1", k), pools[k].at[c], pools[k].at[2 + c], at_z(3),
            when=z != 0 if k in RELAYED else None,
        )
        two = remote(
            ("z2", k), pools[k].at[c], pools[k].at[4 + c], at_z(2),
            when=z != 2 if k in RELAYED else None,
        )
        z_move.append((one, two))
        core_move.append([remote(("c0", k), pools[k].at[c], pools[k].at[c], core)])
    for k in range(AHEAD):
        send_rows(k)
    slab_in = remote(("slab",), h_ref.at[my_rows], slab.at[my_rows, my_cols], across)

    def send_tiles(half):
        return [
            remote(
                ("tile", half, s), c_ref.at[0, 0, s, :, tile_cols(half, ox)],
                tiles[half].at[2 * x + s], across,
            )
            for s in range(2)
        ]

    tile_in = [send_tiles(half) for half in range(1)]

    table_in.wait_recv()
    mine = [t_ref[0, s] for s in range(2)]
    theirs = [jnp.max(tab_in[s]) for s in range(2)]
    first = x == 0
    dist = [jnp.where(first, mine[s], theirs[s]) for s in range(2)]
    dist += [jnp.where(first, theirs[s], mine[s]) for s in range(2)]
    inner = [jnp.logical_and(d != 0, d != half_loop) for d in dist]
    slot_zero = jnp.int32(3)
    slot_half = slot_zero
    for i in range(3):
        slot_zero = jnp.where(dist[i] == 0, i, slot_zero)
        slot_half = jnp.where(dist[i] == half_loop, i, slot_half)
    slot_a = jnp.where(inner[0], 0, jnp.where(inner[1], 1, 2))
    slot_b = jnp.where(inner[3], 3, jnp.where(inner[2], 2, 1))
    inner_slots = (slot_a, slot_b)
    inner_dist = [pick(dist, s) for s in inner_slots]
    own_at = [low + d for d in inner_dist]
    next_at = [low + 2 - 4 * y + d for d in inner_dist]

    def spot(at):
        return (at >> 2) * 2 + (at & 1)

    def here(at):
        return ((at >> 1) & 1) ^ y

    def source(j, plane, side):
        want = plane * 2 + side
        own = jnp.logical_and(here(own_at[j]) == 0, spot(own_at[j]) == want)
        near = jnp.logical_and(here(next_at[j]) == 0, spot(next_at[j]) == want)
        return jnp.where(own, j, jnp.where(near, 2 + j, 4))

    y_move, b_move, b_core, b_z, last = [], [], [], [], []

    def gather_rows(k):
        for step in (1, 2):
            z_move[k][step - 1].wait_recv()
            if step == 1 and k in RELAYED:
                remote(
                    ("via1", k), pools[k].at[2 + c], pools[k].at[4 + c], at_z(3),
                    lands=("z2", k), when=z == 1,
                )
            elif k in RELAYED:
                remote(
                    ("via2", k), pools[k].at[4 + c], pools[k].at[2 + c], at_z(1),
                    lands=("z1", k), when=z == 2,
                )
            core_move[k].append(
                remote(
                    ("c", step, k), pools[k].at[2 * step + c], pools[k].at[2 * step + c], core
                )
            )
        if k + AHEAD < PIECES:
            send_rows(k + AHEAD)
        for copy in core_move[k]:
            copy.wait_recv()
        for j in range(2):
            y_out[k][j] = pools[k][spot(next_at[j])]
        y_move.append(remote(("y", k), y_out[k], sel[k].at[pl.ds(2, 2)], over_y))
        for j in range(2):
            sel[k][j] = pools[k][spot(own_at[j])]

    def compute(k):
        half = k // per_part
        if k == 0:
            for copy in slab_own:
                copy.wait()
            for i in range(PIECES):
                slab[my_chunk(i), other_cols] = pools[i][c, :, other_cols]
            slab_in.wait_recv()
        if k % per_part == 0:
            for copy in tile_in[half]:
                copy.wait_recv()
        stack[pl.ds(0, chunk)] = pools[k][c]
        stack[pl.ds(chunk, chunk)] = pools[k][4 + c]
        y_move[k].wait_recv()
        for j in range(2):
            stack[pl.ds((2 + j) * chunk, chunk)] = sel[k][j + 2 * here(own_at[j])]
        gram = lax.dot_general(
            slab[...], stack[...], (((1,), (1,)), ((), ())), preferred_element_type=f32
        )
        at = (k % per_part) * chunk
        held = jnp.concatenate(
            [tiles[half][s, :, at:at + chunk] for s in (slot_zero, slot_half) + inner_slots],
            axis=1,
        )
        pair = (held.astype(f32) * gram).astype(bf16)
        back = lax.dot_general(
            pair[:, 2 * chunk:], slab[...], (((0,), (0,)), ((), ())), preferred_element_type=f32
        ).astype(bf16)
        for j in range(2):
            cand[k][j] = back[j * chunk:(j + 1) * chunk]
        b_move.append(
            remote(("b", k), cand[k].at[pl.ds(0, 2)], cand[k].at[pl.ds(2, 2)], over_y)
        )
        part = jnp.dot(pair, stack[...], preferred_element_type=f32)
        if k == 0:
            direct[...] = part
        else:
            direct[...] += part
        if k == PIECES - 1:
            d_out[...] = direct[:, other_cols].astype(bf16)
            last.append(remote(("direct",), d_out, d_in, across))

    def sort_back(k):
        b_move[k].wait_recv()
        for plane in (2, 1, 0):
            for side, keep in ((1 - c, False), (c, True)):
                a, b = (cand[k][source(j, plane, side)].astype(f32) for j in range(2))
                if keep:
                    same[k][plane] = a + b
                else:
                    core_out[k][plane] = (a + b).astype(bf16)
        b_core.append(remote(("bc", k), core_out[k], core_in[k], core))

    def send_back(k):
        b_core[k].wait_recv()

        moves = []
        for step in (2, 1, 0):
            z_out[k][step] = (same[k][step] + core_in[k][step].astype(f32)).astype(bf16)
            there = at_z(step)[0]
            moves.append(remote(
                ("far", k, step), z_out[k].at[step, :, other_cols], z_in[k].at[1, step], (there, ox)
            ))
            if step > 0:
                moves.append(remote(
                    ("near", k, step), z_out[k].at[step, :, my_cols], z_in[k].at[0, step], (there, x)
                ))
        b_z.append(moves)

    def finish(k):
        for copy in b_z[k]:
            copy.wait_recv()
        r = my_chunk(k)
        out_ref[r, :] = (
            direct[r, my_cols] + d_in[r, :].astype(f32)
            + same[k][0, :, my_cols] + core_in[k][0, :, my_cols].astype(f32)
            + z_in[k][0, 1].astype(f32) + z_in[k][0, 2].astype(f32)
        ).astype(bf16)
        r = other_chunk(k)
        out_ref[r, :] = (
            direct[r, my_cols] + d_in[r, :].astype(f32) + z_in[k][1, 0].astype(f32)
            + z_in[k][1, 1].astype(f32) + z_in[k][1, 2].astype(f32)
        ).astype(bf16)

    gather_rows(0)
    tile_in.append(send_tiles(1))
    gather_rows(1)
    compute(0)
    gather_rows(2)
    compute(1)
    sort_back(0)
    gather_rows(3)
    send_back(0)
    compute(2)
    sort_back(1)
    send_back(1)
    compute(3)
    sort_back(2)
    send_back(2)
    sort_back(3)
    send_back(3)
    last[0].wait_recv()
    for k in range(PIECES):
        finish(k)

    for copy, when in started:
        if when is None:
            copy.wait_send()
        else:
            pl.when(when)(copy.wait_send)


COPIES = 3 + 2 * PARTS + 18 * PIECES


def planned_body(n_loop, orbitals, coulomb, table):
    points, width = orbitals.shape
    rows, full = points // 2, 2 * width
    chunk = rows // PIECES
    bf16, f32 = jnp.bfloat16, jnp.float32

    def each(shape, dtype=bf16, count=PIECES):
        return [pltpu.VMEM(shape, dtype) for _ in range(count)]

    return pl.pallas_call(
        functools.partial(kernel, n_loop),
        out_shape=jax.ShapeDtypeStruct(orbitals.shape, bf16),
        in_specs=[
            pl.BlockSpec(memory_space=pltpu.HBM),
            pl.BlockSpec(memory_space=pltpu.HBM),
            pl.BlockSpec(memory_space=pltpu.SMEM),
        ],
        out_specs=pl.BlockSpec(memory_space=pltpu.VMEM),
        scratch_shapes=[
            pltpu.VMEM((points, full), bf16),
            each((4, points, rows // PARTS), count=PARTS),
            pltpu.VMEM((2, 8, 128), jnp.int32),
            pltpu.VMEM((2, 8, 128), jnp.int32),
            each((6, chunk, full)),
            each((2, chunk, full)),
            each((4, chunk, full)),
            each((5, chunk, full)),
            each((3, chunk, full), f32),
            each((3, chunk, full)),
            each((3, chunk, full)),
            each((3, chunk, full)),
            each((2, 3, chunk, width)),
            pltpu.VMEM((points, full), f32),
            pltpu.VMEM((points, width), bf16),
            pltpu.VMEM((points, width), bf16),
            pltpu.VMEM((4 * chunk, full), bf16),
            pltpu.SemaphoreType.DMA((COPIES,)),
            pltpu.SemaphoreType.DMA((COPIES,)),
            pltpu.SemaphoreType.DMA((PIECES + 1 + 2 * PARTS,)),
        ],
        compiler_params=pltpu.CompilerParams(
            collective_id=0, has_side_effects=True, vmem_limit_bytes=63 * 1024 * 1024
        ),
    )(orbitals, coulomb, table)


def solution(mesh):
    in_specs = (P("loop", "lane"), P("loop", "lane", None, None, None), P("lane", None))
    out_specs = P("loop", "lane")
    n_loop, n_lane = mesh.shape["loop"], mesh.shape["lane"]
    fits = n_loop == 4 * 4 and n_lane == 2
    body = functools.partial(planned_body, n_loop) if fits else general_body
    return jax.shard_map(body, mesh=mesh, in_specs=in_specs, out_specs=out_specs, check_vma=False)
```
